256 devices in a mesh: layer: 4 (over z_hi, core), example: 64 (over y, x, z_lo).
Axes of the slice: x: 4, y: 4, z: 8 (z_hi: 2, z_lo: 4; z = z_hi * 4 + z_lo), core: 2. Of those that a mesh axis runs over, the one named last changes fastest.
Arguments:
- train_ids: int32 [64, 128], P('example'), may hold values from 0 to 128001, as said below
- query_ids: int32 [512, 16], P('example'), may hold values from 0 to 128001, as said below
- train_acts: bfloat16 [4, 8192, 4096], P('layer', 'example'), may hold values from -6 to 6
- train_contrib: bfloat16 [4, 8192, 4096], P('layer', 'example'), may hold values from -6 to 6
- query_acts: bfloat16 [4, 8192, 4096], P('layer', 'example'), may hold values from -6 to 6
- query_contrib: bfloat16 [4, 8192, 4096], P('layer', 'example'), may hold values from -6 to 6
- in_project: bfloat16 [4, 4096, 64], P('layer'), may hold values from -0.09375 to 0.09375
- out_project: bfloat16 [4, 4096, 64], P('layer'), may hold values from -0.09375 to 0.09375
Outputs:
- scores: float32 [64, 512], P('example', 'layer')
The draws below stay inside these ranges and needn't reach their ends.
Inputs may be any that keep to these rules, and one draw needn't show every extreme that they name: `train_ids`: each row holds a sequence's ids, all below 128001, up to its length, then 128001 to the end; lengths run from 32 to 127. `query_ids`: each row holds a query's ids, all below 128001, up to its length, then 128001 to the end; lengths run from 4 to 15.
All inputs are finite; a program needn't handle non-finite values.
Results may differ from the reference program's by a relative error of at most 0.012.
Values may be sent and summed in bfloat16 or wider, within the bound.
No kernel may reach another device: no remote copies, remote signals or barrier semaphores. Data moves between devices by JAX's collectives and lax.ppermute only.
A program may use at most 128 MiB of HBM per device.

```python
import math
import jax
import jax.numpy as jnp
from jax import lax

D = 4096
K_IN = 64
K_OUT = 64
LEN = 128
QLEN = 16
PAD = 128001
LAYERS = 4
SEQS = 64
QUERIES = 512
TRAIN_TOKENS = 8192
QUERY_TOKENS = 8192


def padded_ids(key, rows, length):
    token_key, length_key = jax.random.split(key)
    tokens = jax.random.randint(token_key, (rows, length), 0, PAD, dtype=jnp.int32)
    ends = jax.random.randint(length_key, (rows, 1), length // 4, length, dtype=jnp.int32)
    position = lax.broadcasted_iota(jnp.int32, (rows, length), 1)
    return jnp.where(position < ends, tokens, jnp.int32(PAD))


def draw_train_ids(key, part):
    key = jax.random.fold_in(key, 5)
    return padded_ids(key, SEQS, LEN)


def draw_query_ids(key, part):
    key = jax.random.fold_in(key, 9)
    return padded_ids(key, QUERIES, QLEN)


def level_of(key, extent, pieces, least, high):
    loudness, own = 1.0, jax.random.fold_in(key, 6)
    for axis_at, parts in pieces:
        steps = jnp.exp(jax.random.uniform(jax.random.fold_in(own, axis_at), (parts,), jnp.float32, least / len(pieces), high / len(pieces)))
        loudness = loudness * jnp.repeat(steps, extent[axis_at] // parts).reshape([-1 if axis == axis_at else 1 for axis in range(len(extent))])
    return loudness


def gaussian(key, dims, spread, limit, cuts=(), kind=jnp.bfloat16):
    drawn = spread * jax.random.normal(key, dims, jnp.float32)
    if cuts:
        drawn = drawn * level_of(key, dims, cuts, -0.22, 0.18)
    return jnp.clip(drawn, -limit, limit).astype(kind)


def setup_inputs(seed: int = 0) -> dict:
    streams_of = jax.random.split(jax.random.key(seed), 9)
    train_ids = draw_train_ids(jax.random.fold_in(streams_of[8], 71), 0)
    query_ids = draw_query_ids(jax.random.fold_in(streams_of[8], 71), 0)
    train_acts = gaussian(streams_of[2], (LAYERS, TRAIN_TOKENS, D), 1.0, 6.0, ((0, 4), (1, 64)))
    train_contrib = gaussian(streams_of[3], (LAYERS, TRAIN_TOKENS, D), 1.0, 6.0, ((0, 4), (1, 64)))
    query_acts = gaussian(streams_of[4], (LAYERS, QUERY_TOKENS, D), 1.0, 6.0, ((0, 4), (1, 64)))
    query_contrib = gaussian(streams_of[5], (LAYERS, QUERY_TOKENS, D), 1.0, 6.0, ((0, 4), (1, 64)))
    in_project = gaussian(streams_of[6], (LAYERS, D, K_IN), D ** -0.5, 0.09375, ((0, 4),))
    out_project = gaussian(streams_of[7], (LAYERS, D, K_OUT), D ** -0.5, 0.09375, ((0, 4),))
    return dict(train_ids=train_ids, query_ids=query_ids, train_acts=train_acts, train_contrib=train_contrib, query_acts=query_acts, query_contrib=query_contrib, in_project=in_project, out_project=out_project)


def example_grads(acts, grads, ids, in_proj, out_proj):
    rows, length = ids.shape
    mask = (ids != PAD).astype(jnp.float32)
    count = lax.optimization_barrier(jnp.sum(mask, axis=1))
    left = jnp.dot(acts, in_proj, preferred_element_type=jnp.float32).reshape(rows, length, -1)
    right = jnp.dot(grads, out_proj.astype(jnp.float32), precision=lax.Precision.HIGHEST).reshape(rows, length, -1)
    right = right * mask[:, :, None]
    outer = jnp.einsum('sti,stj->sij', right, left, precision=lax.Precision.HIGHEST) / count[:, None, None]
    return outer.reshape(rows, -1).astype(jnp.bfloat16)

def reference(train_ids, query_ids, train_acts, train_contrib, query_acts, query_contrib, in_project, out_project):
    running_train = jnp.zeros(train_contrib.shape[1:], jnp.float32)
    running_query = jnp.zeros(query_contrib.shape[1:], jnp.float32)
    total = jnp.zeros((SEQS, QUERIES), jnp.float32)
    for layer_index in reversed(range(LAYERS)):
        running_train = running_train + train_contrib[layer_index].astype(jnp.float32)
        running_query = running_query + query_contrib[layer_index].astype(jnp.float32)
        train_proj = example_grads(train_acts[layer_index], running_train, train_ids, in_project[layer_index], out_project[layer_index])
        query_proj = example_grads(query_acts[layer_index], running_query, query_ids, in_project[layer_index], out_project[layer_index])
        total = total + lax.dot_general(train_proj, query_proj, (((1,), (1,)), ((), ())), preferred_element_type=jnp.float32)
    return total * (1.0 / math.sqrt(K_IN * K_OUT))
```

```python
import math

import jax
import jax.numpy as jnp
from jax import lax
from jax.experimental import pallas as pl
from jax.experimental.pallas import tpu as pltpu
from jax.sharding import Mesh
from jax.sharding import PartitionSpec as P

K_IN = 64
K_OUT = 64
PAD = 128001
D = 4096
SPAN = D // 4
LAYER = ("z_hi", "core")
EXAMPLE = ("y", "x", "z_lo")
PLANE = ("x", "z_lo")
AXES = (("z_hi", 2), ("core", 2), ("y", 4), ("x", 4), ("z_lo", 4))
WIDE = (((1,), (1,)), ((), ()))
PLAIN = (((1,), (0,)), ((), ()))
VMEM = pl.BlockSpec(memory_space=pltpu.VMEM)
SMEM = pl.BlockSpec(memory_space=pltpu.SMEM)
ROOM = pltpu.CompilerParams(vmem_limit_bytes=24 * 1024 * 1024)


def mul(a, b, dims=WIDE, precision=None):
    return lax.dot_general(a, b, dims, precision=precision, preferred_element_type=jnp.float32)


def own_kernel(place, ta, qa, tc, qc, tb, qb, wi, wo, out):
    first = place[1] == 0
    wo_all, wi_all = wo[...], wi[...]
    for k, (own, other) in enumerate(((tc, tb), (qc, qb))):
        here = mul(wo_all, own[...])
        above = mul(wo_all, other[...])
        out[k] = (here + jnp.where(first, above, 0.0)).astype(out.dtype)
    out[2] = mul(wi_all, ta[...]).astype(out.dtype)
    out[3] = mul(wi_all, qa[...]).astype(out.dtype)


def pair_kernel(place, tc, qc, tb, qb, w0, w1, w2, w3, got, tw, qw, train, query):
    x = place[3]
    sums = [got[0].astype(jnp.float32), got[1].astype(jnp.float32)]
    for k, w in enumerate((w0, w1, w2, w3)):
        at = pl.ds(pl.multiple_of(((x - k + 4) % 4) * SPAN, SPAN), SPAN)
        part = w[...]
        for n, (own, other) in enumerate(((tc, tb), (qc, qb))):
            sums[n] += mul(part, own[:, at]) + mul(part, other[:, at])
    right = sums[0] * tw[...]
    outer = mul(right, got[2].astype(jnp.float32), WIDE, lax.Precision.HIGHEST).astype(train.dtype)
    packed = jnp.concatenate([outer[: K_OUT // 2], outer[K_OUT // 2 :]], axis=1)
    train[...] = jnp.broadcast_to(packed[None], train.shape)
    query[0] = (sums[1] * qw[...]).astype(query.dtype)
    query[1] = got[3]


def score_kernel(place, train, q0, q1, q2, q3, out):
    y = place[2]
    slot = place[3] * 4 + place[4]
    half = K_OUT // 2
    token = lax.broadcasted_iota(jnp.int32, (128, 128), 0)
    lane = lax.broadcasted_iota(jnp.int32, (128, 128), 1)
    gather = (lane == slot * 8 + token // 16).astype(jnp.float32)
    stacked = train[...].reshape(16 * half, 2 * K_IN)
    for k, q in enumerate((q0, q1, q2, q3)):
        right, left = q[0].astype(jnp.float32), q[1]
        none = jnp.zeros_like(left)
        low = mul(stacked, jnp.concatenate([left, none], axis=0), PLAIN).reshape(16, half, 128)
        high = mul(stacked, jnp.concatenate([none, left], axis=0), PLAIN).reshape(16, half, 128)
        terms = jnp.sum(low * right[None, :half] + high * right[None, half:], axis=1)
        rows = pl.ds(pl.multiple_of(((y - k + 4) % 4) * 16, 16), 16)
        out[rows, :] = mul(terms, gather, PLAIN, lax.Precision.HIGHEST)


def swap(axis):
    return lambda value: lax.ppermute(value, axis, [(0, 1), (1, 0)])


def shift(value, axis, k):
    return lax.ppermute(value, axis, [(i, (i + k) % 4) for i in range(4)])


def weights(ids):
    mask = (ids != PAD).astype(jnp.float32)
    return (mask / jnp.sum(mask, axis=1, keepdims=True)).reshape(1, -1)


def on_device(
    train_ids,
    query_ids,
    train_acts,
    train_contrib,
    query_acts,
    query_contrib,
    in_project,
    out_project,
):
    place = jnp.stack([lax.axis_index(name) for name, _ in AXES]).astype(jnp.int32)
    tc, qc = train_contrib[0], query_contrib[0]
    wi, wo = in_project[0].T, out_project[0].T
    tb, qb = swap("core")(tc), swap("core")(qc)
    mine = lax.dynamic_slice(wo, (0, lax.axis_index("x") * SPAN), (K_OUT, SPAN))
    w0 = lax.ppermute(mine, "z_hi", [(0, 1)])
    held = pl.pallas_call(
        own_kernel,
        out_shape=jax.ShapeDtypeStruct((4, K_OUT, 128), jnp.bfloat16),
        in_specs=[SMEM] + [VMEM] * 8,
        out_specs=VMEM,
        compiler_params=ROOM,
        name="own",
    )(place, train_acts[0], query_acts[0], tc, qc, tb, qb, wi, wo)
    got = swap("z_hi")(held)
    w1, w2, w3 = (shift(w0, "x", k) for k in (1, 2, 3))
    train, query = pl.pallas_call(
        pair_kernel,
        out_shape=(
            jax.ShapeDtypeStruct((16, K_OUT // 2, 2 * K_IN), jnp.bfloat16),
            jax.ShapeDtypeStruct((2, K_OUT, 128), jnp.bfloat16),
        ),
        in_specs=[SMEM] + [VMEM] * 11,
        out_specs=(VMEM, VMEM),
        compiler_params=ROOM,
        name="pair",
    )(place, tc, qc, tb, qb, w0, w1, w2, w3, got, weights(train_ids), weights(query_ids))
    q1, q2, q3 = (shift(query, "y", k) for k in (1, 2, 3))
    trains = lax.all_to_all(train, PLANE, 0, 0)
    terms = pl.pallas_call(
        score_kernel,
        out_shape=jax.ShapeDtypeStruct((64, 128), jnp.float32),
        in_specs=[SMEM] + [VMEM] * 5,
        out_specs=VMEM,
        compiler_params=ROOM,
        name="score",
    )(place, trains, query, q1, q2, q3)
    landed = lax.all_to_all(terms.reshape(64, 1, 128), LAYER + PLANE, 0, 0)
    return jnp.sum(landed, axis=0) * (1.0 / math.sqrt(K_IN * K_OUT))


def solution(mesh):
    fine = Mesh(mesh.devices.reshape([size for _, size in AXES]), [name for name, _ in AXES])
    placed = (
        P(EXAMPLE, None),
        P(EXAMPLE, None),
        P(LAYER, EXAMPLE, None),
        P(LAYER, EXAMPLE, None),
        P(LAYER, EXAMPLE, None),
        P(LAYER, EXAMPLE, None),
        P(LAYER, None, None),
        P(LAYER, None, None),
    )
    return jax.shard_map(
        on_device, mesh=fine, in_specs=placed, out_specs=P(EXAMPLE, LAYER), check_vma=False
    )
```

```python
import math

import jax
import jax.numpy as jnp
from jax import lax
from jax.experimental import pallas as pl
from jax.experimental.pallas import tpu as pltpu
from jax.sharding import Mesh
from jax.sharding import PartitionSpec as P

K_IN = 64
K_OUT = 64
PAD = 128001
D = 4096
SPAN = D // 4
LAYER = ("z_hi", "core")
EXAMPLE = ("y", "x", "z_lo")
PLANE = ("x", "z_lo")
AXES = (("z_hi", 2), ("core", 2), ("y", 4), ("x", 4), ("z_lo", 4))
WIDE = (((1,), (1,)), ((), ()))
PLAIN = (((1,), (0,)), ((), ()))
HALF = K_OUT // 2
VMEM = pl.BlockSpec(memory_space=pltpu.VMEM)
HBM = pl.BlockSpec(memory_space=pltpu.HBM)
ROOM = pltpu.CompilerParams(vmem_limit_bytes=24 * 1024 * 1024)
OWN_ROOM = pltpu.CompilerParams(vmem_limit_bytes=58 * 1024 * 1024)


def mul(a, b, dims=WIDE, precision=None):
    return lax.dot_general(a, b, dims, precision=precision, preferred_element_type=jnp.float32)


def own_kernel(train_ids, query_ids, ta, qa, tc, qc, tb, qb, wi, wo, held, acts, contribs, weights, sems):
    moves = [
        pltpu.make_async_copy(source, target, sems.at[n])
        for n, (source, target) in enumerate(
            (
                (wi, weights.at[0]),
                (ta, acts.at[pl.ds(0, 128)]),
                (qa, acts.at[pl.ds(128, 128)]),
                (wo, weights.at[1]),
                (tc, contribs.at[pl.ds(0, 128)]),
                (qc, contribs.at[pl.ds(128, 128)]),
                (tb, contribs.at[pl.ds(256, 128)]),
                (qb, contribs.at[pl.ds(384, 128)]),
            )
        )
    ]
    for move in moves:
        move.start()
    mask = (train_ids[...] != PAD).astype(jnp.float32)
    train_weight = mask / jnp.sum(mask, axis=1, keepdims=True)
    mask = (query_ids[...] != PAD).astype(jnp.float32)
    mask = mask / jnp.sum(mask, axis=1, keepdims=True)
    row = lax.broadcasted_iota(jnp.int32, (8, 128), 0)
    lane = lax.broadcasted_iota(jnp.int32, (8, 128), 1)
    spread = jnp.where(lane // 16 == row, jnp.concatenate([mask] * 8, axis=1), 0.0)
    query_weight = jnp.sum(spread, axis=0, keepdims=True)
    for move in moves[:3]:
        move.wait()
    left = mul(acts[...], weights[0])
    left = jnp.concatenate([left[:128], left[128:]], axis=1).T
    held[2] = (left[:K_IN] * train_weight).astype(held.dtype)
    held[3] = (left[K_IN:] * query_weight).astype(held.dtype)
    for move in moves[3:]:
        move.wait()
    right = mul(contribs[...], weights[1])
    right = right[:256] + jnp.where(lax.axis_index("core") == 0, right[256:], 0.0)
    right = jnp.concatenate([right[:128], right[128:]], axis=1).T
    held[0] = right[:K_OUT].astype(held.dtype)
    held[1] = right[K_OUT:].astype(held.dtype)


def pair_kernel(tc, qc, tb, qb, w0, w1, w2, w3, got, train, query):
    x = lax.axis_index("x")
    above = [0.0, 0.0]
    for k, w in enumerate((w0, w1, w2, w3)):
        at = pl.ds(pl.multiple_of(((x - k + 4) % 4) * SPAN, SPAN), SPAN)
        part = w[...]
        for n, (own, other) in enumerate(((tc, tb), (qc, qb))):
            above[n] += mul(own[:, at], part) + mul(other[:, at], part)
    above = jnp.concatenate(above, axis=1).T
    query[0] = (got[1].astype(jnp.float32) + above[K_OUT:]).astype(query.dtype)
    query[1] = got[3]
    right = got[0].astype(jnp.float32) + above[:K_OUT]
    coarse = right.astype(jnp.bfloat16)
    rest = (right - coarse.astype(jnp.float32)).astype(jnp.bfloat16)
    left = got[2]
    outer = mul(jnp.concatenate([coarse, rest], axis=1), jnp.concatenate([left, left], axis=1)).astype(train.dtype)
    packed = jnp.concatenate([outer[:HALF], outer[HALF:]], axis=1)
    train[...] = jnp.broadcast_to(packed[None], train.shape)


def score_kernel(train, q0, q1, q2, q3, out):
    y = lax.axis_index("y")
    slot = lax.axis_index("x") * 4 + lax.axis_index("z_lo")
    token = lax.broadcasted_iota(jnp.int32, (128, 128), 0)
    lane = lax.broadcasted_iota(jnp.int32, (128, 128), 1)
    gather = (lane == slot * 8 + token // 16).astype(jnp.float32)
    stacked = train[...].reshape(16 * HALF, 2 * K_IN)
    for k, q in enumerate((q0, q1, q2, q3)):
        right, left = q[0].astype(jnp.float32), q[1]
        none = jnp.zeros_like(left)
        low = mul(stacked, jnp.concatenate([left, none], axis=0), PLAIN).reshape(16, HALF, 128)
        high = mul(stacked, jnp.concatenate([none, left], axis=0), PLAIN).reshape(16, HALF, 128)
        terms = jnp.sum(low * right[None, :HALF] + high * right[None, HALF:], axis=1)
        rows = pl.ds(pl.multiple_of(((y - k + 4) % 4) * 16, 16), 16)
        out[rows, :] = mul(terms, gather, PLAIN, lax.Precision.HIGHEST)


def swap(axis):
    return lambda value: lax.ppermute(value, axis, [(0, 1), (1, 0)])


def shift(value, axis, k):
    return lax.ppermute(value, axis, [(i, (i + k) % 4) for i in range(4)])


def on_device(
    train_ids,
    query_ids,
    train_acts,
    train_contrib,
    query_acts,
    query_contrib,
    in_project,
    out_project,
):
    tc, qc = train_contrib[0], query_contrib[0]
    wi, wo = in_project[0].T, out_project[0].T
    mine = lax.dynamic_slice(wo, (0, lax.axis_index("x") * SPAN), (K_OUT, SPAN))
    tb, qb = swap("core")(tc), swap("core")(qc)
    w0 = lax.ppermute(mine, "z_hi", [(0, 1)])
    held = pl.pallas_call(
        own_kernel,
        out_shape=jax.ShapeDtypeStruct((4, K_OUT, 128), jnp.bfloat16),
        in_specs=[VMEM] * 2 + [HBM] * 8,
        out_specs=VMEM,
        scratch_shapes=[
            pltpu.VMEM((256, D), jnp.bfloat16),
            pltpu.VMEM((512, D), jnp.bfloat16),
            pltpu.VMEM((2, K_OUT, D), jnp.bfloat16),
            pltpu.SemaphoreType.DMA((8,)),
        ],
        compiler_params=OWN_ROOM,
        name="own",
    )(train_ids, query_ids, train_acts[0], query_acts[0], tc, qc, tb, qb, wi, wo)
    got = swap("z_hi")(held)
    w0, held = lax.optimization_barrier((w0, held))
    w1, w2, w3 = (shift(w0, "x", k) for k in (1, 2, 3))
    train, query = pl.pallas_call(
        pair_kernel,
        out_shape=(
            jax.ShapeDtypeStruct((16, HALF, 2 * K_IN), jnp.bfloat16),
            jax.ShapeDtypeStruct((2, K_OUT, 128), jnp.bfloat16),
        ),
        in_specs=[VMEM] * 9,
        out_specs=(VMEM, VMEM),
        compiler_params=ROOM,
        name="pair",
    )(tc, qc, tb, qb, w0, w1, w2, w3, got)
    q1, q2, q3 = (shift(query, "y", k) for k in (1, 2, 3))
    trains = lax.all_to_all(train, PLANE, 0, 0)
    terms = pl.pallas_call(
        score_kernel,
        out_shape=jax.ShapeDtypeStruct((64, 128), jnp.float32),
        in_specs=[VMEM] * 5,
        out_specs=VMEM,
        compiler_params=ROOM,
        name="score",
    )(trains, query, q1, q2, q3)
    landed = lax.all_to_all(terms.reshape(64, 1, 128), LAYER + PLANE, 0, 0)
    return jnp.sum(landed, axis=0) * (1.0 / math.sqrt(K_IN * K_OUT))


def solution(mesh):
    fine = Mesh(mesh.devices.reshape([size for _, size in AXES]), [name for name, _ in AXES])
    placed = (
        P(EXAMPLE, None),
        P(EXAMPLE, None),
        P(LAYER, EXAMPLE, None),
        P(LAYER, EXAMPLE, None),
        P(LAYER, EXAMPLE, None),
        P(LAYER, EXAMPLE, None),
        P(LAYER, None, None),
        P(LAYER, None, None),
    )
    return jax.shard_map(
        on_device, mesh=fine, in_specs=placed, out_specs=P(EXAMPLE, LAYER), check_vma=False
    )
```

```python
import math

import jax
import jax.numpy as jnp
from jax import lax
from jax.experimental import pallas as pl
from jax.experimental.pallas import tpu as pltpu
from jax.sharding import Mesh
from jax.sharding import PartitionSpec as P

K_IN = 64
K_OUT = 64
PAD = 128001
D = 4096
ROWS = K_OUT // 4
SCALE = 1.0 / math.sqrt(K_IN * K_OUT)
LAYER = ("z_hi", "core")
EXAMPLE = ("y", "x", "z_lo")
PLANE = ("x", "z_lo")
AXES = (("z_hi", 2), ("core", 2), ("y", 4), ("x", 4), ("z_lo", 4))
WIDE = (((1,), (1,)), ((), ()))
PLAIN = (((1,), (0,)), ((), ()))
HALF = K_OUT // 2
VMEM = pl.BlockSpec(memory_space=pltpu.VMEM)
HBM = pl.BlockSpec(memory_space=pltpu.HBM)
ANY = pl.BlockSpec(memory_space=pl.ANY)
ROOM = pltpu.CompilerParams(vmem_limit_bytes=58 * 1024 * 1024)
OWN_ROOM = pltpu.CompilerParams(vmem_limit_bytes=58 * 1024 * 1024)
SMALL = pltpu.CompilerParams(vmem_limit_bytes=16 * 1024 * 1024)


def mul(a, b, dims=WIDE, precision=None):
    return lax.dot_general(a, b, dims, precision=precision, preferred_element_type=jnp.float32)


def copies(pairs, sems):
    moves = [pltpu.make_async_copy(source, target, sems.at[n]) for n, (source, target) in enumerate(pairs)]
    for move in moves:
        move.start()
    return moves


def wait(moves):
    for move in moves:
        move.wait()


def both_sides(product):
    return jnp.concatenate([product[:128], product[128:]], axis=1).T


def token_weights(train_ids, query_ids):
    mask = (train_ids != PAD).astype(jnp.float32)
    train = mask / jnp.sum(mask, axis=1, keepdims=True)
    mask = (query_ids != PAD).astype(jnp.float32)
    mask = mask / jnp.sum(mask, axis=1, keepdims=True)
    row = lax.broadcasted_iota(jnp.int32, (8, 128), 0)
    lane = lax.broadcasted_iota(jnp.int32, (8, 128), 1)
    spaced = jnp.where(lane // 16 == row, jnp.concatenate([mask] * 8, axis=1), 0.0)
    return train, jnp.sum(spaced, axis=0, keepdims=True)


def inputs_of(train, query, products, left):
    both = both_sides(products)
    left[0] = (both[:K_IN] * train).astype(left.dtype)
    left[1] = (both[K_IN:] * query).astype(left.dtype)


def landing(moves, rows, weights):
    halves = []
    for k, move in enumerate(moves):
        move.wait()
        halves.append(mul(rows[pl.ds(k * 128, 128)], weights[...]))
    return jnp.concatenate(halves, axis=0)


def lower_kernel(
    train_ids, query_ids, ta, qa, tc, qc, wi, wo, mine, right, left, acts, contribs, weights, train_row, query_rows, sems
):
    @pl.when(lax.axis_index("z_hi") == 0)
    def _():
        moves = copies(
            (
                (wo, weights.at[1]),
                (tc, contribs.at[pl.ds(0, 128)]),
                (qc, contribs.at[pl.ds(128, 128)]),
                (wi, weights.at[0]),
                (ta, acts.at[pl.ds(0, 128)]),
                (qa, acts.at[pl.ds(128, 128)]),
                (train_ids, train_row),
                (query_ids, query_rows),
            ),
            sems,
        )
        moves[0].wait()
        at = pl.multiple_of((lax.axis_index("x") + lax.axis_index("y")) % 4 * ROWS, ROWS)
        mine[...] = weights[1, pl.ds(at, ROWS), :]
        right[...] = both_sides(landing(moves[1:3], contribs, weights.at[1]))
        wait(moves[6:])
        train, query = token_weights(train_row[...], query_rows[...])
        moves[3].wait()
        inputs_of(train, query, landing(moves[4:6], acts, weights.at[0]), left)


def own_kernel(
    train_ids,
    query_ids,
    ta,
    qa,
    tc,
    qc,
    tb,
    qb,
    wi,
    wo,
    right,
    left,
    held,
    total,
    acts,
    contribs,
    added,
    weights,
    sums,
    train_row,
    query_rows,
    sems,
):
    first = lax.axis_index("core") == 0
    others = ((tb, added.at[pl.ds(0, 128)]), (qb, added.at[pl.ds(128, 128)]))

    @pl.when(lax.axis_index("z_hi") == 0)
    def _():
        moves = copies(((wo, weights.at[1]),) + others + ((right, sums), (left, held.at[pl.ds(2, 2)])), sems)
        moves[0].wait()
        above = both_sides(landing(moves[1:3], added, weights.at[1]))
        wait(moves[3:])
        both = sums[...] + jnp.where(first, above, 0.0)
        held[0] = both[:K_OUT].astype(held.dtype)
        held[1] = both[K_OUT:].astype(held.dtype)

    @pl.when(lax.axis_index("z_hi") == 1)
    def _():
        moves = copies(
            (
                (train_ids, train_row),
                (query_ids, query_rows),
                (wi, weights.at[0]),
                (ta, acts.at[pl.ds(0, 128)]),
                (qa, acts.at[pl.ds(128, 128)]),
                (wo, weights.at[1]),
                (tc, contribs.at[pl.ds(0, 128)]),
                (qc, contribs.at[pl.ds(128, 128)]),
            )
            + others,
            sems,
        )
        wait(moves[:3])
        train, query = token_weights(train_row[...], query_rows[...])
        inputs_of(train, query, landing(moves[3:5], acts, weights.at[0]), held.at[pl.ds(2, 2)])
        wait(moves[5:])
        added[...] = added[...] + contribs[...]
        out = pltpu.make_async_copy(added, total, sems.at[10])
        out.start()

        @pl.when(first)
        def _():
            contribs[...] = added[...]

        both = both_sides(mul(contribs[...], weights[1]))
        held[0] = both[:K_OUT].astype(held.dtype)
        held[1] = both[K_OUT:].astype(held.dtype)
        out.wait()


def pair_kernel(total, w0, w1, w2, w3, got, train, query, weights, sums):
    held = lax.axis_index("x") + lax.axis_index("y")
    sums[...] = jnp.zeros_like(sums)

    @pl.when(lax.axis_index("z_hi") == 1)
    def _():
        for k, w in enumerate((w0, w1, w2, w3)):
            at = pl.ds(pl.multiple_of(((held - k + 4) % 4) * ROWS, ROWS), ROWS)
            weights[at, :] = w[...]
        sums[...] = both_sides(mul(total[...], weights[...]))

    side = (got[1].astype(jnp.float32) + sums[K_OUT:]).astype(query.dtype)
    query[:K_OUT] = side
    query[K_OUT:] = got[3]
    right = got[0].astype(jnp.float32) + sums[:K_OUT]
    coarse = right.astype(jnp.bfloat16)
    rest = (right - coarse.astype(jnp.float32)).astype(jnp.bfloat16)
    left = got[2]
    outer = mul(jnp.concatenate([coarse, rest], axis=1), jnp.concatenate([left, left], axis=1)).astype(train.dtype)
    packed = jnp.concatenate([outer[:HALF], outer[HALF:]], axis=1)
    train[...] = jnp.broadcast_to(packed[None], train.shape)


def score_kernel(train, q0, q1, q2, q3, out):
    y = lax.axis_index("y")
    slot = lax.axis_index("x") * 4 + lax.axis_index("z_lo")
    token = lax.broadcasted_iota(jnp.int32, (128, 128), 0)
    lane = lax.broadcasted_iota(jnp.int32, (128, 128), 1)
    gather = (lane == slot * 8 + token // 16).astype(jnp.float32)
    stacked = train[...].reshape(16 * HALF, 2 * K_IN)
    terms = []
    for q in (q0, q1, q2, q3):
        right, left = q[:K_OUT].astype(jnp.float32), q[K_OUT:]
        none = jnp.zeros_like(left)
        low = mul(stacked, jnp.concatenate([left, none], axis=0), PLAIN).reshape(16, HALF, 128)
        high = mul(stacked, jnp.concatenate([none, left], axis=0), PLAIN).reshape(16, HALF, 128)
        terms.append(jnp.sum(low * right[None, :HALF] + high * right[None, HALF:], axis=1))
    placed = mul(jnp.concatenate(terms, axis=0), gather, PLAIN, lax.Precision.HIGHEST) * SCALE
    for k in range(4):
        out[pl.ds(pl.multiple_of(((y - k + 4) % 4) * 16, 16), 16), :] = placed[16 * k : 16 * k + 16]


def swap(axis):
    return lambda value: lax.ppermute(value, axis, [(0, 1), (1, 0)])


def shift(value, axis, k):
    return lax.ppermute(value, axis, [(i, (i + k) % 4) for i in range(4)])


def spread(value):
    return shift(value, "x", 1), shift(value, "y", 2), shift(value, "x", 3)


def at_once(exchange, value):
    shapes = jax.eval_shape(exchange, value)
    return lax.cond(
        lax.axis_index("core") < 2,
        exchange,
        lambda _: jax.tree.map(lambda part: jnp.zeros(part.shape, part.dtype), shapes),
        value,
    )


def on_device(
    train_ids,
    query_ids,
    train_acts,
    train_contrib,
    query_acts,
    query_contrib,
    in_project,
    out_project,
):
    tc, qc = train_contrib[0], query_contrib[0]
    wi, wo = in_project[0].T, out_project[0].T
    tb, qb = swap("core")(tc), swap("core")(qc)
    whole = (train_ids, query_ids, train_acts[0], query_acts[0], tc, qc)
    mine, right, left = pl.pallas_call(
        lower_kernel,
        out_shape=(
            jax.ShapeDtypeStruct((ROWS, D), jnp.bfloat16),
            jax.ShapeDtypeStruct((2 * K_OUT, 128), jnp.float32),
            jax.ShapeDtypeStruct((2, K_IN, 128), jnp.bfloat16),
        ),
        in_specs=[HBM] * 8,
        out_specs=(VMEM,) * 3,
        scratch_shapes=[
            pltpu.VMEM((256, D), jnp.bfloat16),
            pltpu.VMEM((256, D), jnp.bfloat16),
            pltpu.VMEM((2, K_OUT, D), jnp.bfloat16),
            pltpu.VMEM((1, 128), jnp.int32),
            pltpu.VMEM((8, 16), jnp.int32),
            pltpu.SemaphoreType.DMA((8,)),
        ],
        compiler_params=ROOM,
        name="lower",
    )(*whole, wi, wo)
    w0 = lax.ppermute(mine, "z_hi", [(0, 1)])
    held, total = pl.pallas_call(
        own_kernel,
        out_shape=(
            jax.ShapeDtypeStruct((4, K_OUT, 128), jnp.bfloat16),
            jax.ShapeDtypeStruct((256, D), jnp.bfloat16),
        ),
        in_specs=[HBM] * 6 + [ANY] * 2 + [HBM] * 2 + [ANY] * 2,
        out_specs=(VMEM, HBM),
        scratch_shapes=[
            pltpu.VMEM((256, D), jnp.bfloat16),
            pltpu.VMEM((256, D), jnp.bfloat16),
            pltpu.VMEM((256, D), jnp.bfloat16),
            pltpu.VMEM((2, K_OUT, D), jnp.bfloat16),
            pltpu.VMEM((2 * K_OUT, 128), jnp.float32),
            pltpu.VMEM((1, 128), jnp.int32),
            pltpu.VMEM((8, 16), jnp.int32),
            pltpu.SemaphoreType.DMA((11,)),
        ],
        compiler_params=OWN_ROOM,
        name="own",
    )(*whole, tb, qb, wi, wo, right, left)
    got = swap("z_hi")(held)
    w1, w2, w3 = at_once(spread, w0)
    train, query = pl.pallas_call(
        pair_kernel,
        out_shape=(
            jax.ShapeDtypeStruct((16, HALF, 2 * K_IN), jnp.bfloat16),
            jax.ShapeDtypeStruct((K_OUT + K_IN, 128), jnp.bfloat16),
        ),
        in_specs=[VMEM] * 6,
        out_specs=(VMEM, VMEM),
        scratch_shapes=[
            pltpu.VMEM((K_OUT, D), jnp.bfloat16),
            pltpu.VMEM((2 * K_OUT, 128), jnp.float32),
        ],
        compiler_params=SMALL,
        name="pair",
    )(total, w0, w1, w2, w3, got)
    q1, q2, q3 = (shift(query, "y", k) for k in (1, 2, 3))
    trains = lax.all_to_all(train, PLANE, 0, 0)
    terms = pl.pallas_call(
        score_kernel,
        out_shape=jax.ShapeDtypeStruct((64, 128), jnp.float32),
        in_specs=[VMEM] * 5,
        out_specs=VMEM,
        compiler_params=SMALL,
        name="score",
    )(trains, query, q1, q2, q3)
    landed = lax.all_to_all(terms.reshape(64, 1, 128), LAYER + PLANE, 0, 0)
    return jnp.sum(landed, axis=0)


def solution(mesh):
    fine = Mesh(mesh.devices.reshape([size for _, size in AXES]), [name for name, _ in AXES])
    placed = (
        P(EXAMPLE, None),
        P(EXAMPLE, None),
        P(LAYER, EXAMPLE, None),
        P(LAYER, EXAMPLE, None),
        P(LAYER, EXAMPLE, None),
        P(LAYER, EXAMPLE, None),
        P(LAYER, None, None),
        P(LAYER, None, None),
    )
    return jax.shard_map(
        on_device, mesh=fine, in_specs=placed, out_specs=P(EXAMPLE, LAYER), check_vma=False
    )
```

```python
import math

import jax
import jax.numpy as jnp
from jax import lax
from jax.experimental import pallas as pl
from jax.experimental.pallas import tpu as pltpu
from jax.sharding import Mesh
from jax.sharding import PartitionSpec as P

K_IN = 64
K_OUT = 64
PAD = 128001
D = 4096
ROWS = K_OUT // 4
SCALE = 1.0 / math.sqrt(K_IN * K_OUT)
LAYER = ("z_hi", "core")
EXAMPLE = ("y", "x", "z_lo")
PLANE = ("x", "z_lo")
AXES = (("z_hi", 2), ("core", 2), ("y", 4), ("x", 4), ("z_lo", 4))
WIDE = (((1,), (1,)), ((), ()))
PLAIN = (((1,), (0,)), ((), ()))
HALF = K_OUT // 2
VMEM = pl.BlockSpec(memory_space=pltpu.VMEM)
HBM = pl.BlockSpec(memory_space=pltpu.HBM)
ANY = pl.BlockSpec(memory_space=pl.ANY)
OWN_ROOM = pltpu.CompilerParams(vmem_limit_bytes=59392 * 1024)
LOWER_ROOM = pltpu.CompilerParams(vmem_limit_bytes=59392 * 1024)
PAIR_ROOM = pltpu.CompilerParams(vmem_limit_bytes=24576 * 1024)
SMALL = pltpu.CompilerParams(vmem_limit_bytes=16 * 1024 * 1024)


def mul(a, b, dims=WIDE, precision=None):
    return lax.dot_general(a, b, dims, precision=precision, preferred_element_type=jnp.float32)


def copies(pairs, sems):
    moves = [pltpu.make_async_copy(source, target, sems.at[n]) for n, (source, target) in enumerate(pairs)]
    for move in moves:
        move.start()
    return moves


def wait(moves):
    for move in moves:
        move.wait()


def both_sides(product):
    return jnp.concatenate([product[:128], product[128:]], axis=1).T


def token_weights(train_ids, query_ids):
    mask = (train_ids != PAD).astype(jnp.float32)
    train = mask / jnp.sum(mask, axis=1, keepdims=True)
    mask = (query_ids != PAD).astype(jnp.float32)
    mask = mask / jnp.sum(mask, axis=1, keepdims=True)
    row = lax.broadcasted_iota(jnp.int32, (8, 128), 0)
    lane = lax.broadcasted_iota(jnp.int32, (8, 128), 1)
    spaced = jnp.where(lane // 16 == row, jnp.concatenate([mask] * 8, axis=1), 0.0)
    return train, jnp.sum(spaced, axis=0, keepdims=True)


def inputs_of(train, query, products, left):
    both = both_sides(products)
    left[0] = (both[:K_IN] * train).astype(left.dtype)
    left[1] = (both[K_IN:] * query).astype(left.dtype)


def landing(moves, rows, weights):
    halves = []
    for k, move in enumerate(moves):
        move.wait()
        halves.append(mul(rows[pl.ds(k * 128, 128)], weights[...]))
    return jnp.concatenate(halves, axis=0)


def lower_kernel(
    train_ids, query_ids, ta, qa, tc, qc, wi, wo, mine, right, left, acts, contribs, weights, train_row, query_rows, sems
):
    @pl.when(lax.axis_index("z_hi") == 0)
    def _():
        moves = copies(
            (
                (wo, weights.at[1]),
                (tc, contribs.at[pl.ds(0, 128)]),
                (qc, contribs.at[pl.ds(128, 128)]),
                (wi, weights.at[0]),
                (ta, acts.at[pl.ds(0, 128)]),
                (qa, acts.at[pl.ds(128, 128)]),
                (train_ids, train_row),
                (query_ids, query_rows),
            ),
            sems,
        )
        moves[0].wait()
        at = pl.multiple_of((lax.axis_index("x") + 2 * lax.axis_index("y")) % 4 * ROWS, ROWS)
        mine[...] = weights[1, pl.ds(at, ROWS), :]
        right[...] = both_sides(landing(moves[1:3], contribs, weights.at[1]))
        wait(moves[6:])
        train, query = token_weights(train_row[...], query_rows[...])
        moves[3].wait()
        inputs_of(train, query, landing(moves[4:6], acts, weights.at[0]), left)


def own_kernel(
    train_ids,
    query_ids,
    ta,
    qa,
    tc,
    qc,
    tb,
    qb,
    wi,
    wo,
    right,
    left,
    held,
    total,
    acts,
    contribs,
    added,
    weights,
    sums,
    train_row,
    query_rows,
    sems,
):
    first = lax.axis_index("core") == 0
    others = ((tb, added.at[pl.ds(0, 128)]), (qb, added.at[pl.ds(128, 128)]))

    @pl.when(lax.axis_index("z_hi") == 0)
    def _():
        moves = copies(((wo, weights.at[1]),) + others + ((right, sums), (left, held.at[pl.ds(2, 2)])), sems)
        moves[0].wait()
        above = both_sides(landing(moves[1:3], added, weights.at[1]))
        wait(moves[3:])
        both = sums[...] + jnp.where(first, above, 0.0)
        held[0] = both[:K_OUT].astype(held.dtype)
        held[1] = both[K_OUT:].astype(held.dtype)

    @pl.when(lax.axis_index("z_hi") == 1)
    def _():
        moves = copies(
            (
                (train_ids, train_row),
                (query_ids, query_rows),
                (wi, weights.at[0]),
                (ta, acts.at[pl.ds(0, 128)]),
                (qa, acts.at[pl.ds(128, 128)]),
                (wo, weights.at[1]),
                (tc, contribs.at[pl.ds(0, 128)]),
                (qc, contribs.at[pl.ds(128, 128)]),
            )
            + others,
            sems,
        )
        wait(moves[:3])
        train, query = token_weights(train_row[...], query_rows[...])
        inputs_of(train, query, landing(moves[3:5], acts, weights.at[0]), held.at[pl.ds(2, 2)])
        wait(moves[5:])
        added[...] = added[...] + contribs[...]
        out = pltpu.make_async_copy(added, total, sems.at[10])
        out.start()

        @pl.when(first)
        def _():
            contribs[...] = added[...]

        both = both_sides(mul(contribs[...], weights[1]))
        held[0] = both[:K_OUT].astype(held.dtype)
        held[1] = both[K_OUT:].astype(held.dtype)
        out.wait()


def stage_kernel(total, out, sems):
    halves = [pl.ds(k * 128, 128) for k in range(2)]
    wait(copies([(total.at[half], out.at[half]) for half in halves], sems))


def pair_kernel(total, w0, w1, w2, w3, got, train, query, weights, sums, sems):
    quarter = lax.axis_index("x") + 2 * lax.axis_index("y")
    sums[...] = jnp.zeros_like(sums)

    @pl.when(lax.axis_index("z_hi") == 1)
    def _():
        rows = [pl.ds(pl.multiple_of((quarter + 4 - k) % 4 * ROWS, ROWS), ROWS) for k in range(4)]
        wait(copies([(w, weights.at[at]) for w, at in zip((w0, w1, w2, w3), rows)], sems))
        sums[...] = both_sides(mul(total[...], weights[...]))

    side = (got[1].astype(jnp.float32) + sums[K_OUT:]).astype(query.dtype)
    query[:K_OUT] = side
    query[K_OUT:] = got[3]
    right = got[0].astype(jnp.float32) + sums[:K_OUT]
    coarse = right.astype(jnp.bfloat16)
    rest = (right - coarse.astype(jnp.float32)).astype(jnp.bfloat16)
    left = got[2]
    outer = mul(jnp.concatenate([coarse, rest], axis=1), jnp.concatenate([left, left], axis=1)).astype(train.dtype)
    packed = jnp.concatenate([outer[:HALF], outer[HALF:]], axis=1)
    train[...] = jnp.broadcast_to(packed[None], train.shape)


def score_kernel(train, q0, q1, q2, q3, out, mine, sem):
    move = pltpu.make_async_copy(q0, mine, sem)
    move.start()
    y = lax.axis_index("y")
    slot = lax.axis_index("x") * 4 + lax.axis_index("z_lo")
    token = lax.broadcasted_iota(jnp.int32, (128, 128), 0)
    lane = lax.broadcasted_iota(jnp.int32, (128, 128), 1)
    gather = (lane == slot * 8 + token // 16).astype(jnp.float32)
    stacked = train[...].reshape(16 * HALF, 2 * K_IN)
    terms = []
    for k, q in enumerate((q1, q2, q3, mine)):
        if k == 3:
            move.wait()
        right, left = q[:K_OUT].astype(jnp.float32), q[K_OUT:]
        none = jnp.zeros_like(left)
        low = mul(stacked, jnp.concatenate([left, none], axis=0), PLAIN).reshape(16, HALF, 128)
        high = mul(stacked, jnp.concatenate([none, left], axis=0), PLAIN).reshape(16, HALF, 128)
        terms.append(jnp.sum(low * right[None, :HALF] + high * right[None, HALF:], axis=1))
    placed = mul(jnp.concatenate(terms, axis=0), gather, PLAIN, lax.Precision.HIGHEST) * SCALE
    for k in range(4):
        out[pl.ds(pl.multiple_of(((y - k + 3) % 4) * 16, 16), 16), :] = placed[16 * k : 16 * k + 16]


def swap(axis):
    return lambda value: lax.ppermute(value, axis, [(0, 1), (1, 0)])


def shift(value, axis, k):
    return lax.ppermute(value, axis, [(i, (i + k) % 4) for i in range(4)])


def spread(value):
    weights, total = value
    near = pl.pallas_call(
        stage_kernel,
        out_shape=jax.ShapeDtypeStruct(total.shape, total.dtype),
        in_specs=[HBM],
        out_specs=VMEM,
        scratch_shapes=[pltpu.SemaphoreType.DMA((2,))],
        compiler_params=SMALL,
        name="stage",
    )(total)
    return shift(weights, "x", 1), shift(weights, "y", 1), shift(weights, "x", 3), near


def at_once(exchange, value):
    shapes = jax.eval_shape(exchange, value)
    return lax.cond(
        lax.axis_index("core") < 2,
        exchange,
        lambda _: jax.tree.map(lambda part: jnp.zeros(part.shape, part.dtype), shapes),
        value,
    )


def on_device(
    train_ids,
    query_ids,
    train_acts,
    train_contrib,
    query_acts,
    query_contrib,
    in_project,
    out_project,
):
    tc, qc = train_contrib[0], query_contrib[0]
    wi, wo = in_project[0].T, out_project[0].T
    tb, qb = swap("core")(tc), swap("core")(qc)
    whole = (train_ids, query_ids, train_acts[0], query_acts[0], tc, qc)
    mine, right, left = pl.pallas_call(
        lower_kernel,
        out_shape=(
            jax.ShapeDtypeStruct((ROWS, D), jnp.bfloat16),
            jax.ShapeDtypeStruct((2 * K_OUT, 128), jnp.float32),
            jax.ShapeDtypeStruct((2, K_IN, 128), jnp.bfloat16),
        ),
        in_specs=[HBM] * 8,
        out_specs=(VMEM,) * 3,
        scratch_shapes=[
            pltpu.VMEM((256, D), jnp.bfloat16),
            pltpu.VMEM((256, D), jnp.bfloat16),
            pltpu.VMEM((2, K_OUT, D), jnp.bfloat16),
            pltpu.VMEM((1, 128), jnp.int32),
            pltpu.VMEM((8, 16), jnp.int32),
            pltpu.SemaphoreType.DMA((8,)),
        ],
        compiler_params=LOWER_ROOM,
        name="lower",
    )(*whole, wi, wo)
    w0 = lax.ppermute(mine, ("z_hi", "z_lo"), [(k, 7 - k) for k in range(4)])
    held, total = pl.pallas_call(
        own_kernel,
        out_shape=(
            jax.ShapeDtypeStruct((4, K_OUT, 128), jnp.bfloat16),
            jax.ShapeDtypeStruct((256, D), jnp.bfloat16),
        ),
        in_specs=[HBM] * 6 + [ANY] * 2 + [HBM] * 2 + [ANY] * 2,
        out_specs=(VMEM, HBM),
        scratch_shapes=[
            pltpu.VMEM((256, D), jnp.bfloat16),
            pltpu.VMEM((256, D), jnp.bfloat16),
            pltpu.VMEM((256, D), jnp.bfloat16),
            pltpu.VMEM((2, K_OUT, D), jnp.bfloat16),
            pltpu.VMEM((2 * K_OUT, 128), jnp.float32),
            pltpu.VMEM((1, 128), jnp.int32),
            pltpu.VMEM((8, 16), jnp.int32),
            pltpu.SemaphoreType.DMA((11,)),
        ],
        compiler_params=OWN_ROOM,
        name="own",
    )(*whole, tb, qb, wi, wo, right, left)
    got = swap("z_hi")(held)
    w1, w2, w3, near = at_once(spread, (w0, total))
    train, query = pl.pallas_call(
        pair_kernel,
        out_shape=(
            jax.ShapeDtypeStruct((16, HALF, 2 * K_IN), jnp.bfloat16),
            jax.ShapeDtypeStruct((K_OUT + K_IN, 128), jnp.bfloat16),
        ),
        in_specs=[VMEM] + [ANY] * 4 + [VMEM],
        out_specs=(VMEM, VMEM),
        scratch_shapes=[
            pltpu.VMEM((K_OUT, D), jnp.bfloat16),
            pltpu.VMEM((2 * K_OUT, 128), jnp.float32),
            pltpu.SemaphoreType.DMA((4,)),
        ],
        compiler_params=PAIR_ROOM,
        name="pair",
    )(near, w0, w1, w2, w3, got)
    q1, q2, q3 = (shift(query, "y", k) for k in (1, 2, 3))
    trains = lax.all_to_all(train, PLANE, 0, 0)
    terms = pl.pallas_call(
        score_kernel,
        out_shape=jax.ShapeDtypeStruct((64, 128), jnp.float32),
        in_specs=[VMEM, ANY] + [VMEM] * 3,
        out_specs=VMEM,
        scratch_shapes=[pltpu.VMEM((K_OUT + K_IN, 128), jnp.bfloat16), pltpu.SemaphoreType.DMA],
        compiler_params=SMALL,
        name="score",
    )(trains, query, q1, q2, q3)
    landed = lax.all_to_all(terms.reshape(64, 1, 128), LAYER + PLANE, 0, 0)
    return jnp.sum(landed, axis=0)


def solution(mesh):
    fine = Mesh(mesh.devices.reshape([size for _, size in AXES]), [name for name, _ in AXES])
    placed = (
        P(EXAMPLE, None),
        P(EXAMPLE, None),
        P(LAYER, EXAMPLE, None),
        P(LAYER, EXAMPLE, None),
        P(LAYER, EXAMPLE, None),
        P(LAYER, EXAMPLE, None),
        P(LAYER, None, None),
        P(LAYER, None, None),
    )
    return jax.shard_map(
        on_device, mesh=fine, in_specs=placed, out_specs=P(EXAMPLE, LAYER), check_vma=False
    )
```

```python
import math

import jax
import jax.numpy as jnp
from jax import lax
from jax.experimental import pallas as pl
from jax.experimental.pallas import tpu as pltpu
from jax.sharding import Mesh
from jax.sharding import PartitionSpec as P

K_IN = 64
K_OUT = 64
PAD = 128001
D = 4096
ROWS = K_OUT // 4
SCALE = 1.0 / math.sqrt(K_IN * K_OUT)
LAYER = ("z_hi", "core")
EXAMPLE = ("y", "x", "z_lo")
PLANE = ("x", "z_lo")
AXES = (("z_hi", 2), ("core", 2), ("y", 4), ("x", 4), ("z_lo", 4))
WIDE = (((1,), (1,)), ((), ()))
PLAIN = (((1,), (0,)), ((), ()))
HALF = K_OUT // 2
VMEM = pl.BlockSpec(memory_space=pltpu.VMEM)
HBM = pl.BlockSpec(memory_space=pltpu.HBM)
ANY = pl.BlockSpec(memory_space=pl.ANY)
OWN_ROOM = pltpu.CompilerParams(vmem_limit_bytes=54681 * 1024)
LOWER_ROOM = pltpu.CompilerParams(vmem_limit_bytes=54681 * 1024)
PAIR_ROOM = pltpu.CompilerParams(vmem_limit_bytes=24576 * 1024)
SMALL = pltpu.CompilerParams(vmem_limit_bytes=16 * 1024 * 1024)


def mul(a, b, dims=WIDE, precision=None):
    return lax.dot_general(a, b, dims, precision=precision, preferred_element_type=jnp.float32)


def copies(pairs, sems):
    moves = [pltpu.make_async_copy(source, target, sems.at[n]) for n, (source, target) in enumerate(pairs)]
    for move in moves:
        move.start()
    return moves


def wait(moves):
    for move in moves:
        move.wait()


def both_sides(product):
    return jnp.concatenate([product[:128], product[128:]], axis=1).T


def token_weights(train_ids, query_ids):
    mask = (train_ids != PAD).astype(jnp.float32)
    train = mask / jnp.sum(mask, axis=1, keepdims=True)
    mask = (query_ids != PAD).astype(jnp.float32)
    mask = mask / jnp.sum(mask, axis=1, keepdims=True)
    row = lax.broadcasted_iota(jnp.int32, (8, 128), 0)
    lane = lax.broadcasted_iota(jnp.int32, (8, 128), 1)
    spaced = jnp.where(lane // 16 == row, jnp.concatenate([mask] * 8, axis=1), 0.0)
    return train, jnp.sum(spaced, axis=0, keepdims=True)


def inputs_of(train, query, both, left):
    left[0] = (both[:K_IN] * train).astype(left.dtype)
    left[1] = (both[K_IN:] * query).astype(left.dtype)


def landing(moves, rows, weights):
    halves = []
    for k, move in enumerate(moves):
        move.wait()
        halves.append(mul(rows[pl.ds(k * 128, 128)], weights[...]))
    return jnp.concatenate(halves, axis=0)


def lower_kernel(ta, qa, tc, qc, wi, wo, mine, right, left, acts, contribs, weights, sems):
    @pl.when(lax.axis_index("z_hi") == 0)
    def _():
        moves = copies(
            (
                (wo, weights.at[1]),
                (tc, contribs.at[pl.ds(0, 128)]),
                (qc, contribs.at[pl.ds(128, 128)]),
                (wi, weights.at[0]),
                (ta, acts.at[pl.ds(0, 128)]),
                (qa, acts.at[pl.ds(128, 128)]),
            ),
            sems,
        )
        moves[0].wait()
        at = pl.multiple_of((lax.axis_index("x") + 2 * lax.axis_index("y")) % 4 * ROWS, ROWS)
        mine[...] = weights[1, pl.ds(at, ROWS), :]
        right[...] = both_sides(landing(moves[1:3], contribs, weights.at[1]))
        moves[3].wait()
        left[...] = both_sides(landing(moves[4:6], acts, weights.at[0]))


def own_kernel(
    train_ids,
    query_ids,
    ta,
    qa,
    tc,
    qc,
    tb,
    qb,
    wi,
    wo,
    right,
    left,
    held,
    total,
    acts,
    contribs,
    added,
    weights,
    train_row,
    query_rows,
    sems,
):
    first = lax.axis_index("core") == 0
    others = ((tb, added.at[pl.ds(0, 128)]), (qb, added.at[pl.ds(128, 128)]))

    @pl.when(lax.axis_index("z_hi") == 0)
    def _():
        moves = copies(((wo, weights.at[1]),) + others + ((train_ids, train_row), (query_ids, query_rows)), sems)
        wait(moves[3:])
        train, query = token_weights(train_row[...], query_rows[...])
        inputs_of(train, query, left[...], held.at[pl.ds(2, 2)])
        moves[0].wait()
        above = both_sides(landing(moves[1:3], added, weights.at[1]))
        both = right[...] + jnp.where(first, above, 0.0)
        held[0] = both[:K_OUT].astype(held.dtype)
        held[1] = both[K_OUT:].astype(held.dtype)

    @pl.when(lax.axis_index("z_hi") == 1)
    def _():
        moves = copies(
            (
                (train_ids, train_row),
                (query_ids, query_rows),
                (wi, weights.at[0]),
                (ta, acts.at[pl.ds(0, 128)]),
                (qa, acts.at[pl.ds(128, 128)]),
                (wo, weights.at[1]),
                (tc, contribs.at[pl.ds(0, 128)]),
                (qc, contribs.at[pl.ds(128, 128)]),
            )
            + others,
            sems,
        )
        wait(moves[:3])
        train, query = token_weights(train_row[...], query_rows[...])
        inputs_of(train, query, both_sides(landing(moves[3:5], acts, weights.at[0])), held.at[pl.ds(2, 2)])
        wait(moves[5:])
        added[...] = added[...] + contribs[...]
        out = pltpu.make_async_copy(added, total, sems.at[10])
        out.start()

        @pl.when(first)
        def _():
            contribs[...] = added[...]

        both = both_sides(mul(contribs[...], weights[1]))
        held[0] = both[:K_OUT].astype(held.dtype)
        held[1] = both[K_OUT:].astype(held.dtype)
        out.wait()


def stage_kernel(total, out, sems):
    halves = [pl.ds(k * 128, 128) for k in range(2)]
    wait(copies([(total.at[half], out.at[half]) for half in halves], sems))


def pair_kernel(total, w0, w1, w2, w3, got, train, query, weights, sums, sems):
    quarter = lax.axis_index("x") + 2 * lax.axis_index("y")
    sums[...] = jnp.zeros_like(sums)

    @pl.when(lax.axis_index("z_hi") == 1)
    def _():
        rows = [pl.ds(pl.multiple_of((quarter + 4 - k) % 4 * ROWS, ROWS), ROWS) for k in range(4)]
        wait(copies([(w, weights.at[at]) for w, at in zip((w0, w1, w2, w3), rows)], sems))
        above = mul(weights[...], total[...])
        sums[:K_OUT] = above[:, :128]
        sums[K_OUT:] = above[:, 128:]

    side = (got[1].astype(jnp.float32) + sums[K_OUT:]).astype(query.dtype)
    query[:K_OUT] = side
    query[K_OUT:] = got[3]
    right = got[0].astype(jnp.float32) + sums[:K_OUT]
    coarse = right.astype(jnp.bfloat16)
    rest = (right - coarse.astype(jnp.float32)).astype(jnp.bfloat16)
    left = got[2]
    outer = mul(jnp.concatenate([coarse, rest], axis=1), jnp.concatenate([left, left], axis=1)).astype(train.dtype)
    packed = jnp.concatenate([outer[:HALF], outer[HALF:]], axis=1)
    train[...] = jnp.broadcast_to(packed[None], train.shape)


def score_kernel(train, q0, q1, q2, q3, out, mine, sem):
    move = pltpu.make_async_copy(q0, mine, sem)
    move.start()
    y = lax.axis_index("y")
    slot = lax.axis_index("x") * 4 + lax.axis_index("z_lo")
    token = lax.broadcasted_iota(jnp.int32, (128, 128), 0)
    lane = lax.broadcasted_iota(jnp.int32, (128, 128), 1)
    gather = (lane == slot * 8 + token // 16).astype(jnp.float32)
    stacked = train[...].reshape(16 * HALF, 2 * K_IN)
    terms = []
    for k, q in enumerate((q1, q2, q3, mine)):
        if k == 3:
            move.wait()
        right, left = q[:K_OUT].astype(jnp.float32), q[K_OUT:]
        none = jnp.zeros_like(left)
        low = mul(stacked, jnp.concatenate([left, none], axis=0), PLAIN).reshape(16, HALF, 128)
        high = mul(stacked, jnp.concatenate([none, left], axis=0), PLAIN).reshape(16, HALF, 128)
        terms.append(jnp.sum(low * right[None, :HALF] + high * right[None, HALF:], axis=1))
    placed = mul(jnp.concatenate(terms, axis=0), gather, PLAIN, lax.Precision.HIGHEST) * SCALE
    for k in range(4):
        out[pl.ds(pl.multiple_of(((y - k + 3) % 4) * 16, 16), 16), :] = placed[16 * k : 16 * k + 16]


def swap(axis):
    return lambda value: lax.ppermute(value, axis, [(0, 1), (1, 0)])


def shift(value, axis, k):
    return lax.ppermute(value, axis, [(i, (i + k) % 4) for i in range(4)])


def spread(value):
    weights, total = value
    near = pl.pallas_call(
        stage_kernel,
        out_shape=jax.ShapeDtypeStruct(total.shape, total.dtype),
        in_specs=[HBM],
        out_specs=VMEM,
        scratch_shapes=[pltpu.SemaphoreType.DMA((2,))],
        compiler_params=SMALL,
        name="stage",
    )(total)
    return shift(weights, "x", 1), shift(weights, "y", 1), shift(weights, "x", 3), near


def at_once(exchange, value):
    shapes = jax.eval_shape(exchange, value)
    return lax.cond(
        lax.axis_index("core") < 2,
        exchange,
        lambda _: jax.tree.map(lambda part: jnp.zeros(part.shape, part.dtype), shapes),
        value,
    )


def on_device(
    train_ids,
    query_ids,
    train_acts,
    train_contrib,
    query_acts,
    query_contrib,
    in_project,
    out_project,
):
    tc, qc = train_contrib[0], query_contrib[0]
    wi, wo = in_project[0].T, out_project[0].T
    tb, qb = swap("core")(tc), swap("core")(qc)
    whole = (train_ids, query_ids, train_acts[0], query_acts[0], tc, qc)
    mine, right, left = pl.pallas_call(
        lower_kernel,
        out_shape=(
            jax.ShapeDtypeStruct((ROWS, D), jnp.bfloat16),
            jax.ShapeDtypeStruct((2 * K_OUT, 128), jnp.float32),
            jax.ShapeDtypeStruct((2 * K_IN, 128), jnp.float32),
        ),
        in_specs=[HBM] * 6,
        out_specs=(VMEM,) * 3,
        scratch_shapes=[
            pltpu.VMEM((256, D), jnp.bfloat16),
            pltpu.VMEM((256, D), jnp.bfloat16),
            pltpu.VMEM((2, K_OUT, D), jnp.bfloat16),
            pltpu.SemaphoreType.DMA((6,)),
        ],
        compiler_params=LOWER_ROOM,
        name="lower",
    )(*whole[2:], wi, wo)
    w0 = lax.ppermute(mine, ("z_hi", "z_lo"), [(k, 7 - k) for k in range(4)])
    held, total = pl.pallas_call(
        own_kernel,
        out_shape=(
            jax.ShapeDtypeStruct((4, K_OUT, 128), jnp.bfloat16),
            jax.ShapeDtypeStruct((256, D), jnp.bfloat16),
        ),
        in_specs=[HBM] * 6 + [ANY] * 2 + [HBM] * 2 + [VMEM] * 2,
        out_specs=(VMEM, HBM),
        scratch_shapes=[
            pltpu.VMEM((256, D), jnp.bfloat16),
            pltpu.VMEM((256, D), jnp.bfloat16),
            pltpu.VMEM((256, D), jnp.bfloat16),
            pltpu.VMEM((2, K_OUT, D), jnp.bfloat16),
            pltpu.VMEM((1, 128), jnp.int32),
            pltpu.VMEM((8, 16), jnp.int32),
            pltpu.SemaphoreType.DMA((11,)),
        ],
        compiler_params=OWN_ROOM,
        name="own",
    )(*whole, tb, qb, wi, wo, right, left)
    got = swap("z_hi")(held)
    w1, w2, w3, near = at_once(spread, (w0, total))
    train, query = pl.pallas_call(
        pair_kernel,
        out_shape=(
            jax.ShapeDtypeStruct((16, HALF, 2 * K_IN), jnp.bfloat16),
            jax.ShapeDtypeStruct((K_OUT + K_IN, 128), jnp.bfloat16),
        ),
        in_specs=[VMEM] + [ANY] * 4 + [VMEM],
        out_specs=(VMEM, VMEM),
        scratch_shapes=[
            pltpu.VMEM((K_OUT, D), jnp.bfloat16),
            pltpu.VMEM((2 * K_OUT, 128), jnp.float32),
            pltpu.SemaphoreType.DMA((4,)),
        ],
        compiler_params=PAIR_ROOM,
        name="pair",
    )(near, w0, w1, w2, w3, got)
    q1, q2, q3 = (shift(query, "y", k) for k in (1, 2, 3))
    trains = lax.all_to_all(train, PLANE, 0, 0)
    terms = pl.pallas_call(
        score_kernel,
        out_shape=jax.ShapeDtypeStruct((64, 128), jnp.float32),
        in_specs=[VMEM, ANY] + [VMEM] * 3,
        out_specs=VMEM,
        scratch_shapes=[pltpu.VMEM((K_OUT + K_IN, 128), jnp.bfloat16), pltpu.SemaphoreType.DMA],
        compiler_params=SMALL,
        name="score",
    )(trains, query, q1, q2, q3)
    landed = lax.all_to_all(terms.reshape(64, 1, 128), LAYER + PLANE, 0, 0)
    return jnp.sum(landed, axis=0)


def solution(mesh):
    fine = Mesh(mesh.devices.reshape([size for _, size in AXES]), [name for name, _ in AXES])
    placed = (
        P(EXAMPLE, None),
        P(EXAMPLE, None),
        P(LAYER, EXAMPLE, None),
        P(LAYER, EXAMPLE, None),
        P(LAYER, EXAMPLE, None),
        P(LAYER, EXAMPLE, None),
        P(LAYER, None, None),
        P(LAYER, None, None),
    )
    return jax.shard_map(
        on_device, mesh=fine, in_specs=placed, out_specs=P(EXAMPLE, LAYER), check_vma=False
    )
```

```python
import math

import jax
import jax.numpy as jnp
from jax import lax
from jax.experimental import pallas as pl
from jax.experimental.pallas import tpu as pltpu
from jax.sharding import Mesh
from jax.sharding import PartitionSpec as P

K_IN = 64
K_OUT = 64
PAD = 128001
D = 4096
ROWS = K_OUT // 4
SCALE = 1.0 / math.sqrt(K_IN * K_OUT)
LAYER = ("z_hi", "core")
EXAMPLE = ("y", "x", "z_lo")
PLANE = ("x", "z_lo")
AXES = (("z_hi", 2), ("core", 2), ("y", 4), ("x", 4), ("z_lo", 4))
WIDE = (((1,), (1,)), ((), ()))
PLAIN = (((1,), (0,)), ((), ()))
HALF = K_OUT // 2
VMEM = pl.BlockSpec(memory_space=pltpu.VMEM)
HBM = pl.BlockSpec(memory_space=pltpu.HBM)
ANY = pl.BlockSpec(memory_space=pl.ANY)
SEND_ROOM = pltpu.CompilerParams(vmem_limit_bytes=54681 * 1024)
SMALL = pltpu.CompilerParams(vmem_limit_bytes=16 * 1024 * 1024)


def mul(a, b, dims=WIDE, precision=None):
    return lax.dot_general(a, b, dims, precision=precision, preferred_element_type=jnp.float32)


def copies(pairs, sems):
    moves = [pltpu.make_async_copy(source, target, sems.at[n]) for n, (source, target) in enumerate(pairs)]
    for move in moves:
        move.start()
    return moves


def wait(moves):
    for move in moves:
        move.wait()


def both_sides(product):
    return jnp.concatenate([product[:128], product[128:]], axis=1).T


def token_weights(train_ids, query_ids):
    mask = (train_ids != PAD).astype(jnp.float32)
    train = mask / jnp.sum(mask, axis=1, keepdims=True)
    mask = (query_ids != PAD).astype(jnp.float32)
    mask = mask / jnp.sum(mask, axis=1, keepdims=True)
    row = lax.broadcasted_iota(jnp.int32, (8, 128), 0)
    lane = lax.broadcasted_iota(jnp.int32, (8, 128), 1)
    spaced = jnp.where(lane // 16 == row, jnp.concatenate([mask] * 8, axis=1), 0.0)
    return train, jnp.sum(spaced, axis=0, keepdims=True)


def send_kernel(wo, mine, sem):
    @pl.when(lax.axis_index("z_hi") == 0)
    def _():
        at = pl.multiple_of((lax.axis_index("x") + 2 * lax.axis_index("y")) % 4 * ROWS, ROWS)
        move = pltpu.make_async_copy(wo.at[pl.ds(at, ROWS)], mine, sem)
        move.start()
        move.wait()


def own_kernel(train_ids, query_ids, ta, qa, tc, qc, tb, qb, wi, wo, held, total, chosen):
    train, query = token_weights(train_ids[...], query_ids[...])
    left = both_sides(jnp.concatenate([mul(ta[...], wi[...]), mul(qa[...], wi[...])], axis=0))
    held[2] = (left[:K_IN] * train).astype(held.dtype)
    held[3] = (left[K_IN:] * query).astype(held.dtype)
    total[:128] = tc[...] + tb[...]
    total[128:] = qc[...] + qb[...]
    first = lax.axis_index("core") == 0

    @pl.when(first)
    def _():
        chosen[...] = total[...]

    @pl.when(jnp.logical_not(first))
    def _():
        chosen[:128] = tc[...]
        chosen[128:] = qc[...]

    right = both_sides(mul(chosen[...], wo[...]))
    held[0] = right[:K_OUT].astype(held.dtype)
    held[1] = right[K_OUT:].astype(held.dtype)


def pair_kernel(total, w0, w1, w2, w3, got, train, query, weights, sums, sems):
    quarter = lax.axis_index("x") + 2 * lax.axis_index("y")
    sums[...] = jnp.zeros_like(sums)

    @pl.when(lax.axis_index("z_hi") == 1)
    def _():
        rows = [pl.ds(pl.multiple_of((quarter + 4 - k) % 4 * ROWS, ROWS), ROWS) for k in range(4)]
        wait(copies([(w, weights.at[at]) for w, at in zip((w0, w1, w2, w3), rows)], sems))
        above = mul(weights[...], total[...])
        sums[:K_OUT] = above[:, :128]
        sums[K_OUT:] = above[:, 128:]

    side = (got[1].astype(jnp.float32) + sums[K_OUT:]).astype(query.dtype)
    query[:K_OUT] = side
    query[K_OUT:] = got[3]
    right = got[0].astype(jnp.float32) + sums[:K_OUT]
    coarse = right.astype(jnp.bfloat16)
    rest = (right - coarse.astype(jnp.float32)).astype(jnp.bfloat16)
    left = got[2]
    outer = mul(jnp.concatenate([coarse, rest], axis=1), jnp.concatenate([left, left], axis=1)).astype(train.dtype)
    packed = jnp.concatenate([outer[:HALF], outer[HALF:]], axis=1)
    train[...] = jnp.broadcast_to(packed[None], train.shape)


def score_kernel(train, q0, q1, q2, q3, out, mine, sem):
    move = pltpu.make_async_copy(q0, mine, sem)
    move.start()
    y = lax.axis_index("y")
    slot = lax.axis_index("x") * 4 + lax.axis_index("z_lo")
    token = lax.broadcasted_iota(jnp.int32, (128, 128), 0)
    lane = lax.broadcasted_iota(jnp.int32, (128, 128), 1)
    gather = (lane == slot * 8 + token // 16).astype(jnp.float32)
    stacked = train[...].reshape(16 * HALF, 2 * K_IN)
    terms = []
    for k, q in enumerate((q1, q2, q3, mine)):
        if k == 3:
            move.wait()
        right, left = q[:K_OUT].astype(jnp.float32), q[K_OUT:]
        none = jnp.zeros_like(left)
        low = mul(stacked, jnp.concatenate([left, none], axis=0), PLAIN).reshape(16, HALF, 128)
        high = mul(stacked, jnp.concatenate([none, left], axis=0), PLAIN).reshape(16, HALF, 128)
        terms.append(jnp.sum(low * right[None, :HALF] + high * right[None, HALF:], axis=1))
    placed = mul(jnp.concatenate(terms, axis=0), gather, PLAIN, lax.Precision.HIGHEST) * SCALE
    for k in range(4):
        out[pl.ds(pl.multiple_of(((y - k + 3) % 4) * 16, 16), 16), :] = placed[16 * k : 16 * k + 16]


def swap(axis):
    return lambda value: lax.ppermute(value, axis, [(0, 1), (1, 0)])


def shift(value, axis, k):
    return lax.ppermute(value, axis, [(i, (i + k) % 4) for i in range(4)])


def spread(value):
    return shift(value, "x", 1), shift(value, "y", 1), shift(value, "x", 3)


def at_once(exchange, value):
    shapes = jax.eval_shape(exchange, value)
    return lax.cond(
        lax.axis_index("core") < 2,
        exchange,
        lambda _: jax.tree.map(lambda part: jnp.zeros(part.shape, part.dtype), shapes),
        value,
    )


def on_device(
    train_ids,
    query_ids,
    train_acts,
    train_contrib,
    query_acts,
    query_contrib,
    in_project,
    out_project,
):
    tc, qc = train_contrib[0], query_contrib[0]
    wi, wo = in_project[0].T, out_project[0].T
    tb, qb = swap("core")(tc), swap("core")(qc)
    mine = pl.pallas_call(
        send_kernel,
        out_shape=jax.ShapeDtypeStruct((ROWS, D), jnp.bfloat16),
        in_specs=[HBM],
        out_specs=VMEM,
        scratch_shapes=[pltpu.SemaphoreType.DMA],
        compiler_params=SEND_ROOM,
        cost_estimate=pl.CostEstimate(flops=20000000000, bytes_accessed=1 << 20, transcendentals=0),
        name="send",
    )(wo)
    w0 = lax.ppermute(mine, ("z_hi", "z_lo"), [(k, 7 - k) for k in range(4)])
    held, total = pl.pallas_call(
        own_kernel,
        out_shape=(
            jax.ShapeDtypeStruct((4, K_OUT, 128), jnp.bfloat16),
            jax.ShapeDtypeStruct((256, D), jnp.bfloat16),
        ),
        in_specs=[VMEM] * 10,
        out_specs=(VMEM, VMEM),
        scratch_shapes=[pltpu.VMEM((256, D), jnp.bfloat16)],
        compiler_params=SMALL,
        name="own",
    )(train_ids, query_ids, train_acts[0], query_acts[0], tc, qc, tb, qb, wi, wo)
    got = swap("z_hi")(held)
    w1, w2, w3 = at_once(spread, w0)
    train, query = pl.pallas_call(
        pair_kernel,
        out_shape=(
            jax.ShapeDtypeStruct((16, HALF, 2 * K_IN), jnp.bfloat16),
            jax.ShapeDtypeStruct((K_OUT + K_IN, 128), jnp.bfloat16),
        ),
        in_specs=[VMEM] + [ANY] * 4 + [VMEM],
        out_specs=(VMEM, VMEM),
        scratch_shapes=[
            pltpu.VMEM((K_OUT, D), jnp.bfloat16),
            pltpu.VMEM((2 * K_OUT, 128), jnp.float32),
            pltpu.SemaphoreType.DMA((4,)),
        ],
        compiler_params=SMALL,
        name="pair",
    )(total, w0, w1, w2, w3, got)
    q1, q2, q3 = (shift(query, "y", k) for k in (1, 2, 3))
    trains = lax.all_to_all(train, PLANE, 0, 0)
    terms = pl.pallas_call(
        score_kernel,
        out_shape=jax.ShapeDtypeStruct((64, 128), jnp.float32),
        in_specs=[VMEM, ANY] + [VMEM] * 3,
        out_specs=VMEM,
        scratch_shapes=[pltpu.VMEM((K_OUT + K_IN, 128), jnp.bfloat16), pltpu.SemaphoreType.DMA],
        compiler_params=SMALL,
        name="score",
    )(trains, query, q1, q2, q3)
    landed = lax.all_to_all(terms.reshape(64, 1, 128), LAYER + PLANE, 0, 0)
    return jnp.sum(landed, axis=0)


def solution(mesh):
    fine = Mesh(mesh.devices.reshape([size for _, size in AXES]), [name for name, _ in AXES])
    placed = (
        P(EXAMPLE, None),
        P(EXAMPLE, None),
        P(LAYER, EXAMPLE, None),
        P(LAYER, EXAMPLE, None),
        P(LAYER, EXAMPLE, None),
        P(LAYER, EXAMPLE, None),
        P(LAYER, None, None),
        P(LAYER, None, None),
    )
    return jax.shard_map(
        on_device, mesh=fine, in_specs=placed, out_specs=P(EXAMPLE, LAYER), check_vma=False
    )
```

```python
import math

import jax
import jax.numpy as jnp
from jax import lax
from jax.experimental import pallas as pl
from jax.experimental.pallas import tpu as pltpu
from jax.sharding import Mesh
from jax.sharding import PartitionSpec as P

K_IN = 64
K_OUT = 64
PAD = 128001
D = 4096
ROWS = K_OUT // 4
SCALE = 1.0 / math.sqrt(K_IN * K_OUT)
LAYER = ("z_hi", "core")
EXAMPLE = ("y", "x", "z_lo")
PLANE = ("x", "z_lo")
AXES = (("z_hi", 2), ("core", 2), ("y", 4), ("x", 4), ("z_lo", 4))
WIDE = (((1,), (1,)), ((), ()))
PLAIN = (((1,), (0,)), ((), ()))
HALF = K_OUT // 2
VMEM = pl.BlockSpec(memory_space=pltpu.VMEM)
HBM = pl.BlockSpec(memory_space=pltpu.HBM)
ANY = pl.BlockSpec(memory_space=pl.ANY)
SEND_ROOM = pltpu.CompilerParams(vmem_limit_bytes=54681 * 1024)
SMALL = pltpu.CompilerParams(vmem_limit_bytes=16 * 1024 * 1024)


def mul(a, b, dims=WIDE, precision=None):
    return lax.dot_general(a, b, dims, precision=precision, preferred_element_type=jnp.float32)


def copies(pairs, sems):
    moves = [pltpu.make_async_copy(source, target, sems.at[n]) for n, (source, target) in enumerate(pairs)]
    for move in moves:
        move.start()
    return moves


def wait(moves):
    for move in moves:
        move.wait()


def both_sides(product):
    return jnp.concatenate([product[:128], product[128:]], axis=1).T


def token_weights(train_ids, query_ids):
    mask = (train_ids != PAD).astype(jnp.float32)
    train = mask / jnp.sum(mask, axis=1, keepdims=True)
    mask = (query_ids != PAD).astype(jnp.float32)
    mask = mask / jnp.sum(mask, axis=1, keepdims=True)
    row = lax.broadcasted_iota(jnp.int32, (8, 128), 0)
    lane = lax.broadcasted_iota(jnp.int32, (8, 128), 1)
    spaced = jnp.where(lane // 16 == row, jnp.concatenate([mask] * 8, axis=1), 0.0)
    return train, jnp.sum(spaced, axis=0, keepdims=True)


def send_kernel(wo, mine, sem):
    @pl.when(lax.axis_index("z_hi") == 0)
    def _():
        at = pl.multiple_of((lax.axis_index("x") + 2 * lax.axis_index("y")) % 4 * ROWS, ROWS)
        move = pltpu.make_async_copy(wo.at[pl.ds(at, ROWS)], mine, sem)
        move.start()
        move.wait()

    @pl.when(lax.axis_index("z_hi") == 1)
    def _():
        mine[...] = jnp.zeros_like(mine)


def own_kernel(train_ids, query_ids, ta, qa, tc, qc, tb, qb, wi, wo, held, total, chosen):
    train, query = token_weights(train_ids[...], query_ids[...])
    left = both_sides(jnp.concatenate([mul(ta[...], wi[...]), mul(qa[...], wi[...])], axis=0))
    held[2] = (left[:K_IN] * train).astype(held.dtype)
    held[3] = (left[K_IN:] * query).astype(held.dtype)
    total[:128] = tc[...] + tb[...]
    total[128:] = qc[...] + qb[...]
    first = lax.axis_index("core") == 0

    @pl.when(first)
    def _():
        chosen[...] = total[...]

    @pl.when(jnp.logical_not(first))
    def _():
        chosen[:128] = tc[...]
        chosen[128:] = qc[...]

    right = both_sides(mul(chosen[...], wo[...]))
    held[0] = right[:K_OUT].astype(held.dtype)
    held[1] = right[K_OUT:].astype(held.dtype)


def pair_kernel(total, w0, w1, w2, w3, got, train, query, weights, sums, sems):
    quarter = lax.axis_index("x") + 2 * lax.axis_index("y")
    sums[...] = jnp.zeros_like(sums)

    @pl.when(lax.axis_index("z_hi") == 1)
    def _():
        rows = [pl.ds(pl.multiple_of((quarter + 4 - k) % 4 * ROWS, ROWS), ROWS) for k in range(4)]
        wait(copies([(w, weights.at[at]) for w, at in zip((w0, w1, w2, w3), rows)], sems))
        above = mul(weights[...], total[...])
        sums[:K_OUT] = above[:, :128]
        sums[K_OUT:] = above[:, 128:]

    side = (got[1].astype(jnp.float32) + sums[K_OUT:]).astype(query.dtype)
    query[:K_OUT] = side
    query[K_OUT:] = got[3]
    right = got[0].astype(jnp.float32) + sums[:K_OUT]
    coarse = right.astype(jnp.bfloat16)
    rest = (right - coarse.astype(jnp.float32)).astype(jnp.bfloat16)
    left = got[2]
    outer = mul(jnp.concatenate([coarse, rest], axis=1), jnp.concatenate([left, left], axis=1)).astype(train.dtype)
    packed = jnp.concatenate([outer[:HALF], outer[HALF:]], axis=1)
    train[...] = jnp.broadcast_to(packed[None], train.shape)


def score_kernel(train, q0, q1, q2, q3, out, mine, sem):
    move = pltpu.make_async_copy(q0, mine, sem)
    move.start()
    y = lax.axis_index("y")
    slot = lax.axis_index("x") * 4 + lax.axis_index("z_lo")
    token = lax.broadcasted_iota(jnp.int32, (128, 128), 0)
    lane = lax.broadcasted_iota(jnp.int32, (128, 128), 1)
    gather = (lane == slot * 8 + token // 16).astype(jnp.float32)
    stacked = train[...].reshape(16 * HALF, 2 * K_IN)
    terms = []
    for k, q in enumerate((q1, q2, q3, mine)):
        if k == 3:
            move.wait()
        right, left = q[:K_OUT].astype(jnp.float32), q[K_OUT:]
        none = jnp.zeros_like(left)
        low = mul(stacked, jnp.concatenate([left, none], axis=0), PLAIN).reshape(16, HALF, 128)
        high = mul(stacked, jnp.concatenate([none, left], axis=0), PLAIN).reshape(16, HALF, 128)
        terms.append(jnp.sum(low * right[None, :HALF] + high * right[None, HALF:], axis=1))
    placed = mul(jnp.concatenate(terms, axis=0), gather, PLAIN, lax.Precision.HIGHEST) * SCALE
    for k in range(4):
        out[pl.ds(pl.multiple_of(((y - k + 3) % 4) * 16, 16), 16), :] = placed[16 * k : 16 * k + 16]


def swap(axis):
    return lambda value: lax.ppermute(value, axis, [(0, 1), (1, 0)])


def shift(value, axis, k):
    return lax.ppermute(value, axis, [(i, (i + k) % 4) for i in range(4)])


def spread(value):
    return shift(value, "x", 1), shift(value, "y", 1), shift(value, "x", 3)


def at_once(exchange, value):
    shapes = jax.eval_shape(exchange, value)
    return lax.cond(
        lax.axis_index("core") < 2,
        exchange,
        lambda _: jax.tree.map(lambda part: jnp.zeros(part.shape, part.dtype), shapes),
        value,
    )


def on_device(
    train_ids,
    query_ids,
    train_acts,
    train_contrib,
    query_acts,
    query_contrib,
    in_project,
    out_project,
):
    tc, qc = train_contrib[0], query_contrib[0]
    wi, wo = in_project[0].T, out_project[0].T
    tb, qb = swap("core")(tc), swap("core")(qc)
    mine = pl.pallas_call(
        send_kernel,
        out_shape=jax.ShapeDtypeStruct((ROWS, D), jnp.bfloat16),
        in_specs=[HBM],
        out_specs=VMEM,
        scratch_shapes=[pltpu.SemaphoreType.DMA],
        compiler_params=SEND_ROOM,
        cost_estimate=pl.CostEstimate(flops=20000000000, bytes_accessed=1 << 20, transcendentals=0),
        name="send",
    )(wo)
    w0 = lax.ppermute(mine, ("z_hi", "z_lo"), [(k, 7 - k) for k in range(8)])
    held, total = pl.pallas_call(
        own_kernel,
        out_shape=(
            jax.ShapeDtypeStruct((4, K_OUT, 128), jnp.bfloat16),
            jax.ShapeDtypeStruct((256, D), jnp.bfloat16),
        ),
        in_specs=[VMEM] * 10,
        out_specs=(VMEM, VMEM),
        scratch_shapes=[pltpu.VMEM((256, D), jnp.bfloat16)],
        compiler_params=SMALL,
        name="own",
    )(train_ids, query_ids, train_acts[0], query_acts[0], tc, qc, tb, qb, wi, wo)
    got = swap("z_hi")(held)
    w1, w2, w3 = at_once(spread, w0)
    train, query = pl.pallas_call(
        pair_kernel,
        out_shape=(
            jax.ShapeDtypeStruct((16, HALF, 2 * K_IN), jnp.bfloat16),
            jax.ShapeDtypeStruct((K_OUT + K_IN, 128), jnp.bfloat16),
        ),
        in_specs=[VMEM] + [ANY] * 4 + [VMEM],
        out_specs=(VMEM, VMEM),
        scratch_shapes=[
            pltpu.VMEM((K_OUT, D), jnp.bfloat16),
            pltpu.VMEM((2 * K_OUT, 128), jnp.float32),
            pltpu.SemaphoreType.DMA((4,)),
        ],
        compiler_params=SMALL,
        name="pair",
    )(total, w0, w1, w2, w3, got)
    q1, q2, q3 = (shift(query, "y", k) for k in (1, 2, 3))
    trains = lax.all_to_all(train, PLANE, 0, 0)
    terms = pl.pallas_call(
        score_kernel,
        out_shape=jax.ShapeDtypeStruct((64, 128), jnp.float32),
        in_specs=[VMEM, ANY] + [VMEM] * 3,
        out_specs=VMEM,
        scratch_shapes=[pltpu.VMEM((K_OUT + K_IN, 128), jnp.bfloat16), pltpu.SemaphoreType.DMA],
        compiler_params=SMALL,
        name="score",
    )(trains, query, q1, q2, q3)
    landed = lax.all_to_all(terms.reshape(64, 1, 128), LAYER + PLANE, 0, 0)
    return jnp.sum(landed, axis=0)


def solution(mesh):
    fine = Mesh(mesh.devices.reshape([size for _, size in AXES]), [name for name, _ in AXES])
    placed = (
        P(EXAMPLE, None),
        P(EXAMPLE, None),
        P(LAYER, EXAMPLE, None),
        P(LAYER, EXAMPLE, None),
        P(LAYER, EXAMPLE, None),
        P(LAYER, EXAMPLE, None),
        P(LAYER, None, None),
        P(LAYER, None, None),
    )
    return jax.shard_map(
        on_device, mesh=fine, in_specs=placed, out_specs=P(EXAMPLE, LAYER), check_vma=False
    )
```
